32 devices in a mesh: groups: 2 (over x), gx: 8 (over z, y), gy: 2 (over core).
Axes of the slice: x: 2, y: 2, z: 4, core: 2. Of those that a mesh axis runs over, the one named last changes fastest.
Arguments:
- hidden_state_rows: bfloat16 [384, 16384], P(('groups', 'gx'), 'gy'), parts along dimension 0, may hold values from -6 to 6
- base_projection_weight: bfloat16 [16384, 16384], P('gx', 'gy'), may hold values from -0.046875 to 0.046875
- adapter_down_weight: bfloat16 [16384, 64, 16], P('gy', 'gx'), may hold values from -0.046875 to 0.046875
- adapter_up_weight: bfloat16 [64, 16, 16384], P('gx', None, 'gy'), may hold values from -1.5 to 1.5
- adapter_index_rows: int32 [384], P(('groups', 'gx')), parts along dimension 0, may hold values from 0 to 63, as said below
Outputs:
- projected: bfloat16 [384, 16384], P(('groups', 'gx'), 'gy'), parts along dimension 0
The draws below stay inside these ranges and needn't reach their ends.
There are 2 independent parts, one for each index of `groups`. The reference program is written for one: setup_inputs(seed, part) draws one part's arguments, and reference() takes and returns one part's arrays. A program takes and returns all parts, laid end to end along the dimension named above; an argument that names none is the same for every part. Nothing has to cross between parts.
Inputs may be any that keep to these rules, and one draw needn't show every extreme that they name: `adapter_index_rows`: adapter a belongs to owner a // 8. In each aligned block of 24 rows, no owner's adapters are named by more than 6 rows, and in every block some owner's adapters are named by exactly 6 rows.
All inputs are finite; a program needn't handle non-finite values.
Results may differ from the reference program's by a relative error of at most 0.014.
Values may be sent and summed in bfloat16 or wider, within the bound.
A program may use at most 128 MiB of HBM per device.

```python
import jax
import jax.numpy as jnp
from jax import lax

MODEL_WIDTH = 16384
ADAPTER_RANK = 16
ADP_DEV = 8
ROW_DEV = 24
CAP = 6
ROWS = 192
ADAPTER_COUNT = 64
N_GX = 8


def block_owners(block_key):
    key_perm, key_shuffle = jax.random.split(block_key, 2)
    slot_order = jax.random.permutation(key_perm, N_GX * CAP).astype(jnp.int32)
    slot_owner = slot_order // CAP
    first_owner = slot_owner[0]
    is_first = (slot_owner == first_owner).astype(jnp.int32)
    others = slot_owner[jnp.argsort(is_first, stable=True)]
    owner_rows = jnp.concatenate([jnp.full((CAP,), first_owner, jnp.int32), others[:ROW_DEV - CAP]])
    shuffle = jax.random.permutation(key_shuffle, ROW_DEV).astype(jnp.int32)
    return owner_rows[shuffle]


def draw_adapter_index_rows(key, part):
    key = jax.random.fold_in(key, 7)
    key_blocks, key_local = jax.random.split(key, 2)
    owners = jax.vmap(block_owners)(jax.random.split(key_blocks, N_GX))
    local_pick = jax.random.randint(key_local, (N_GX, ROW_DEV), 0, ADP_DEV)
    return (owners * ADP_DEV + local_pick).reshape(ROWS).astype(jnp.int32)


def block_scale(own_key, shape, cuts, least, top_value):
    factor_of, own = 1.0, jax.random.fold_in(own_key, 6)
    for dim, shards_of in cuts:
        steps = jnp.exp(jax.random.uniform(jax.random.fold_in(own, dim), (shards_of,), jnp.float32, least / len(cuts), top_value / len(cuts)))
        factor_of = factor_of * jnp.repeat(steps, shape[dim] // shards_of).reshape([-1 if axis == dim else 1 for axis in range(len(shape))])
    return factor_of


def gaussian(stream_key, dims, scale, bound, cuts=(), kind=jnp.bfloat16):
    array = scale * jax.random.normal(stream_key, dims, jnp.float32)
    if cuts:
        array = array * block_scale(stream_key, dims, cuts, -0.22, 0.18)
    return jnp.clip(array, -bound, bound).astype(kind)


def setup_inputs(seed: int = 0, part: int = 0) -> dict:
    keys = jax.random.split(jax.random.key(seed), 6)
    part_keys = jax.random.split(jax.random.fold_in(keys[5], part), 6)
    return {
        "hidden_state_rows": gaussian(part_keys[0], (ROWS, MODEL_WIDTH), 1.0, 6.0, ((0, 8), (1, 2))),
        "base_projection_weight": gaussian(keys[1], (MODEL_WIDTH, MODEL_WIDTH), MODEL_WIDTH ** -0.5, 0.046875, ((0, 8), (1, 2))),
        "adapter_down_weight": gaussian(keys[2], (MODEL_WIDTH, ADAPTER_COUNT, ADAPTER_RANK), MODEL_WIDTH ** -0.5, 0.046875, ((0, 2), (1, 8))),
        "adapter_up_weight": gaussian(keys[3], (ADAPTER_COUNT, ADAPTER_RANK, MODEL_WIDTH), ADAPTER_RANK ** -0.5, 1.5, ((0, 8), (2, 2))),
        "adapter_index_rows": draw_adapter_index_rows(jax.random.fold_in(jax.random.fold_in(keys[5], part), 71), part),
    }


UPDATE_SCALE = 0.5


def reference(hidden_state_rows, base_projection_weight, adapter_down_weight, adapter_up_weight, adapter_index_rows):
    tile_width = MODEL_WIDTH // N_GX

    def tile_sum(total, tile_index):
        first_column = (tile_index * tile_width).astype(jnp.int32)
        columns = lax.dynamic_slice_in_dim(hidden_state_rows, first_column, tile_width, 1)
        weights = lax.dynamic_slice_in_dim(base_projection_weight, first_column, tile_width, 0)
        partial_sum = jnp.dot(columns, weights, preferred_element_type=jnp.float32).astype(jnp.bfloat16)
        partial_sum = lax.optimization_barrier(partial_sum)
        return total + partial_sum.astype(jnp.float32), None

    base_total, unused = lax.scan(tile_sum, jnp.zeros((ROWS, MODEL_WIDTH), jnp.float32), jnp.arange(N_GX, dtype=jnp.int32))

    def one_row(packed_row):
        row_values, adapter_choice_each = packed_row
        adapter_choice_each = adapter_choice_each.astype(jnp.int32)
        down_weight_rows = lax.dynamic_index_in_dim(adapter_down_weight, adapter_choice_each, 1, keepdims=False)
        rank_reduce_step = jnp.dot(row_values[None, :], down_weight_rows, preferred_element_type=jnp.float32).astype(jnp.bfloat16)
        expand_step_output = lax.dynamic_index_in_dim(adapter_up_weight, adapter_choice_each, 0, keepdims=False)
        update_row_single = (UPDATE_SCALE * jnp.dot(rank_reduce_step, expand_step_output, preferred_element_type=jnp.float32)).astype(jnp.bfloat16)
        return update_row_single[0]

    deltas = lax.map(one_row, (hidden_state_rows, adapter_index_rows))
    return (base_total + deltas.astype(jnp.float32)).astype(jnp.bfloat16)
```

```python
import functools

import jax
import jax.numpy as jnp
from jax import lax
from jax.experimental import pallas as pl
from jax.experimental.pallas import tpu as pltpu
from jax.sharding import PartitionSpec as P

UPDATE_SCALE = 0.5
FOLD = 8
ROW_PAD = 32
MESH = pl.DeviceIdType.MESH
F32 = jnp.float32
BF16 = jnp.bfloat16


def kernel(
    n, capacity, rank, chunks,
    ids_ref, hid_ref, w_ref, down_ref, up_ref, out_ref,
    w_v, down_v, up_v, ids_all, tile_in, rows, folded, packed, slots_in,
    half_out, half_in, part, y_in, z_in,
    w_sem, ad_sem, id_send, id_recv, t_send, t_recv, f_send, l_send, l_recv,
    h_send, h_recv, y_send, y_recv, z_send, z_recv,
):
    g, c, s = lax.axis_index("groups"), lax.axis_index("gx"), lax.axis_index("gy")
    m = n // 2
    zz, yy = c // 2, c % 2
    row_dev, width = hid_ref.shape
    tile = w_ref.shape[0]
    fold_width = width // FOLD
    slot_rows = capacity * FOLD
    cc = width // chunks
    primary = (c // m) == s

    def peer(cx):
        return (g, cx, s)

    partner = (g, c, 1 - s)

    def w_copy(k):
        cols = pl.ds(pl.multiple_of(k * cc, cc), cc)
        return pltpu.make_async_copy(w_ref.at[:, cols], w_v.at[:, cols], w_sem.at[k])

    down_copy = pltpu.make_async_copy(down_ref, down_v, ad_sem.at[0])
    up_copy = pltpu.make_async_copy(up_ref, up_v, ad_sem.at[1])

    barrier = pltpu.get_barrier_semaphore()
    for j in range(1, n):
        pl.semaphore_signal(barrier, inc=1, device_id=peer((c + j) % n), device_id_type=MESH)
    pl.semaphore_signal(barrier, inc=1, device_id=partner, device_id_type=MESH)

    @pl.loop(0, chunks)
    def _(k):
        w_copy(k).start()

    down_copy.start()
    up_copy.start()

    pl.semaphore_wait(barrier, n)

    def id_copy(dst, j):
        return pltpu.make_async_remote_copy(
            ids_ref, ids_all.at[c], id_send.at[j], id_recv.at[c], device_id=peer(dst),
            device_id_type=MESH,
        )

    def tile_copy(j):
        t = s * m + j
        cols = pl.ds(pl.multiple_of(j * tile, tile), tile)
        return t, pltpu.make_async_remote_copy(
            hid_ref.at[:, cols], tile_in.at[c], t_send.at[j], t_recv.at[c],
            device_id=peer(t), device_id_type=MESH,
        )

    own_cols = pl.ds(pl.multiple_of((c - s * m) * tile, tile), tile)

    @pl.loop(0, m)
    def _(j):
        t, copy = tile_copy(j)

        @pl.when(t != c)
        def _():
            copy.start()

    @pl.when(primary)
    def _():
        pltpu.make_async_copy(hid_ref.at[:, own_cols], tile_in.at[c], t_recv.at[c]).start()

    @pl.loop(1, n)
    def _(j):
        id_copy((c + j) % n, j).start()

    own_ids = pltpu.make_async_copy(ids_ref, ids_all.at[c], id_recv.at[c])
    own_ids.start()

    k_pad = FOLD * ROW_PAD
    owner_row = ids_ref[1:2, :]
    lane = lax.broadcasted_iota(jnp.int32, (ROW_PAD, k_pad), 1)
    sub = lax.broadcasted_iota(jnp.int32, (ROW_PAD, k_pad), 0)
    owner_all = jnp.broadcast_to(owner_row, (ROW_PAD, k_pad))
    owner_col = jnp.sum(jnp.where(lane == sub, owner_all, 0.0), axis=1, keepdims=True)
    earlier = (owner_all == owner_col) & (sub < (lane & (ROW_PAD - 1)))
    rank_row = jnp.sum(jnp.where(earlier, 1.0, 0.0), axis=0, keepdims=True)
    code_row = jnp.where(owner_row >= 0.0, owner_row * capacity + rank_row, -1.0)
    code_row = code_row.astype(jnp.int32)
    total_rows = n * slot_rows
    big_row = lax.broadcasted_iota(jnp.int32, (total_rows, k_pad), 0)
    big_lane = lax.broadcasted_iota(jnp.int32, (total_rows, k_pad), 1)
    placer = ((big_row >> 3) == code_row) & ((big_row & 7) == (big_lane >> 5))
    placer = jnp.where(placer, 1.0, 0.0).astype(BF16)
    for q in range(FOLD):
        block = hid_ref[:, q * fold_width:(q + 1) * fold_width].astype(F32)
        block = jnp.concatenate(
            [block, jnp.zeros((ROW_PAD - row_dev, fold_width), F32)], axis=0
        )
        folded[q * ROW_PAD:(q + 1) * ROW_PAD, :] = block.astype(BF16)
    sent = jnp.dot(placer, folded[...], preferred_element_type=F32).astype(BF16)
    for d in range(n):
        packed[d] = sent[d * slot_rows:(d + 1) * slot_rows, :]

    def slot_copy(dst, j):
        return pltpu.make_async_remote_copy(
            packed.at[dst], slots_in.at[c], l_send.at[j], l_recv.at[c], device_id=peer(dst),
            device_id_type=MESH,
        )

    @pl.loop(1, n)
    def _(j):
        slot_copy((c + j) % n, j).start()

    own_slots = pltpu.make_async_copy(packed.at[c], slots_in.at[c], l_recv.at[c])
    own_slots.start()

    def forward(src):
        return pltpu.make_async_remote_copy(
            tile_in.at[src], tile_in.at[src], f_send.at[src], t_recv.at[src],
            device_id=partner, device_id_type=MESH,
        )

    @pl.loop(0, n)
    def _(j):
        src = (c + j) % n
        forward(src).wait_recv()

        @pl.when(primary)
        def _():
            forward(src).start()

    for p in range(m):
        pair = jnp.concatenate([tile_in[2 * p].astype(F32), tile_in[2 * p + 1].astype(F32)], axis=0)
        rows[2 * row_dev * p:2 * row_dev * (p + 1), :] = pair.astype(BF16)

    def columns(k):
        return pl.ds(pl.multiple_of(k * cc, cc), cc)

    @pl.loop(0, chunks)
    def _(k):
        w_copy(k).wait()
        cols = columns(k)
        acc = jnp.dot(rows[...], w_v[:, cols], preferred_element_type=F32)
        for b in range(n):
            part[b % 2, b // 2, :, cols] = acc[b * row_dev:(b + 1) * row_dev, :].astype(BF16)

    @pl.loop(1, n)
    def _(j):
        src = (c + j) % n
        pltpu.make_async_remote_copy(
            packed.at[src], slots_in.at[src], l_send.at[j], l_recv.at[src],
            device_id=peer(src), device_id_type=MESH,
        ).wait_recv()

    own_slots.wait()
    down_copy.wait()
    slots = slots_in[...].reshape(total_rows, fold_width)
    cols_rank = down_ref.shape[1]
    fold_of = lax.broadcasted_iota(jnp.int32, (total_rows, cols_rank), 0) & 7
    low = jnp.zeros((total_rows, cols_rank), F32)
    for q in range(FOLD):
        term = jnp.dot(
            slots, down_v[q * fold_width:(q + 1) * fold_width, :], preferred_element_type=F32
        )
        low = low + jnp.where(fold_of == q, term, 0.0)
    slot_total = n * capacity
    half = jnp.sum(low.reshape(slot_total, FOLD, cols_rank), axis=1)
    half_out[...] = half
    half_copy = pltpu.make_async_remote_copy(
        half_out, half_in, h_send, h_recv, device_id=partner, device_id_type=MESH
    )
    half_copy.start()

    @pl.loop(1, n)
    def _(j):
        src = (c + j) % n
        pltpu.make_async_remote_copy(
            ids_ref, ids_all.at[src], id_send.at[j], id_recv.at[src], device_id=peer(src),
            device_id_type=MESH,
        ).wait_recv()

    own_ids.wait()
    hit_list, id_list = [], []
    sub = lax.broadcasted_iota(jnp.int32, (row_dev, 128), 0)
    lane = lax.broadcasted_iota(jnp.int32, (row_dev, 128), 1)
    slot_lane = lax.broadcasted_iota(jnp.int32, (row_dev, slot_total), 1).astype(F32)
    me = c.astype(F32)
    for b in range(n):
        id_row = jnp.broadcast_to(ids_all[b, 0:1, 0:128], (row_dev, 128))
        owner_row = jnp.broadcast_to(ids_all[b, 1:2, 0:128], (row_dev, 128))
        id_col = jnp.sum(jnp.where(lane == sub, id_row, 0.0), axis=1, keepdims=True)
        owner_col = jnp.sum(jnp.where(lane == sub, owner_row, 0.0), axis=1, keepdims=True)
        earlier = (owner_row == owner_col) & (lane < sub)
        rank_col = jnp.sum(jnp.where(earlier, 1.0, 0.0), axis=1, keepdims=True)
        slot_col = jnp.where(owner_col == me, b * capacity + rank_col, -1.0)
        hit_list.append(jnp.where(slot_lane == slot_col, 1.0, 0.0))
        id_list.append(jnp.broadcast_to(id_col, (row_dev, cols_rank)))
    hits = jnp.concatenate(hit_list, axis=0).astype(BF16)
    ids = jnp.concatenate(id_list, axis=0)
    half_copy.wait()
    shrink = (half + half_in[...]).astype(BF16)
    spread = jnp.dot(hits, shrink, preferred_element_type=F32)
    first = (lax.broadcasted_iota(jnp.int32, ids.shape, 1) + c * cols_rank).astype(F32)
    off = first - rank * ids
    low_rows = jnp.where((off >= 0.0) & (off < rank), spread * UPDATE_SCALE, 0.0).astype(BF16)

    up_copy.wait()

    def y_copy(k):
        cols = columns(k)
        return pltpu.make_async_remote_copy(
            part.at[1 - yy, :, :, cols], y_in.at[:, :, cols], y_send.at[k], y_recv.at[k],
            device_id=peer(zz * 2 + 1 - yy), device_id_type=MESH,
        )

    @pl.loop(0, chunks)
    def _(k):
        cols = columns(k)
        acc = jnp.dot(low_rows, up_v[:, cols], preferred_element_type=F32)
        for b in range(n):
            one = acc[b * row_dev:(b + 1) * row_dev, :]
            part[b % 2, b // 2, :, cols] = (part[b % 2, b // 2, :, cols].astype(F32) + one).astype(BF16)
        y_copy(k).start()

    def z_copy(k, j):
        to = (zz + j) % m
        cols = columns(k)
        return pltpu.make_async_remote_copy(
            part.at[yy, to, :, cols], z_in.at[zz, :, cols], z_send.at[k, j], z_recv.at[k, zz],
            device_id=peer(to * 2 + yy), device_id_type=MESH,
        )

    @pl.loop(0, chunks)
    def _(k):
        cols = columns(k)
        y_copy(k).wait_recv()
        for b in range(m):
            total = part[yy, b, :, cols].astype(F32) + y_in[b, :, cols].astype(F32)
            part[yy, b, :, cols] = total.astype(BF16)

        @pl.loop(1, m)
        def _(j):
            z_copy(k, j).start()

    @pl.loop(0, chunks)
    def _(k):
        cols = columns(k)
        total = part[yy, zz, :, cols].astype(F32)
        for j in range(1, m):
            src = (zz + j) % m
            pltpu.make_async_remote_copy(
                part.at[yy, src, :, cols], z_in.at[src, :, cols], z_send.at[k, j],
                z_recv.at[k, src], device_id=peer(src * 2 + yy), device_id_type=MESH,
            ).wait_recv()
            total = total + z_in[src, :, cols].astype(F32)
        out_ref[:, cols] = total.astype(out_ref.dtype)

    @pl.loop(0, chunks)
    def _(k):
        y_copy(k).wait_send()

        @pl.loop(1, m)
        def _(j):
            z_copy(k, j).wait_send()

    @pl.loop(1, n)
    def _(j):
        id_copy((c + j) % n, j).wait_send()
        slot_copy((c + j) % n, j).wait_send()

    @pl.loop(0, m)
    def _(j):
        t, copy = tile_copy(j)

        @pl.when(t != c)
        def _():
            copy.wait_send()

    @pl.when(primary)
    def _():
        @pl.loop(0, n)
        def _(src):
            forward(src).wait_send()


def on_device(n, hidden, base, down, up, index):
    row_dev, width = hidden.shape
    tile = base.shape[0]
    per_owner, rank = up.shape[0], up.shape[1]
    joined = per_owner * rank
    down = down.reshape(width, joined)
    up = up.reshape(joined, width)
    capacity = max(2, 2 * row_dev // n)
    chunks = 8
    m = n // 2
    padded = jnp.pad(index, (0, ROW_PAD - row_dev), constant_values=-1)
    owner = jnp.where(padded < 0, -1, padded // per_owner)
    first = (jnp.arange(8) == 0)[:, None]
    ids = jnp.where(first, jnp.tile(padded, FOLD)[None, :], jnp.tile(owner, FOLD)[None, :])
    ids = ids.astype(F32)
    slot_rows = capacity * FOLD
    dma = pltpu.SemaphoreType.DMA
    vmem = pl.BlockSpec(memory_space=pltpu.VMEM)
    anywhere = pl.BlockSpec(memory_space=pl.ANY)
    rows_all = n * row_dev
    return pl.pallas_call(
        functools.partial(kernel, n, capacity, rank, chunks),
        out_shape=jax.ShapeDtypeStruct((row_dev, width), BF16),
        in_specs=[vmem, vmem, anywhere, anywhere, anywhere],
        out_specs=vmem,
        scratch_shapes=[
            pltpu.VMEM((tile, width), BF16),
            pltpu.VMEM((width, joined), BF16),
            pltpu.VMEM((joined, width), BF16),
            pltpu.VMEM((n, 8, FOLD * ROW_PAD), F32),
            pltpu.VMEM((n, row_dev, tile), BF16),
            pltpu.VMEM((rows_all, tile), BF16),
            pltpu.VMEM((FOLD * ROW_PAD, width // FOLD), BF16),
            pltpu.VMEM((n, slot_rows, width // FOLD), BF16),
            pltpu.VMEM((n, slot_rows, width // FOLD), BF16),
            pltpu.VMEM((n * capacity, joined), F32),
            pltpu.VMEM((n * capacity, joined), F32),
            pltpu.VMEM((2, m, row_dev, width), BF16),
            pltpu.VMEM((m, row_dev, width), BF16),
            pltpu.VMEM((m, row_dev, width), BF16),
            dma((chunks,)),
            dma((2,)),
            dma((n,)), dma((n,)),
            dma((m,)), dma((n,)),
            dma((n,)),
            dma((n,)), dma((n,)),
            dma, dma,
            dma((chunks,)), dma((chunks,)),
            dma((chunks, m)), dma((chunks, m)),
        ],
        compiler_params=pltpu.CompilerParams(
            collective_id=0, has_side_effects=True, vmem_limit_bytes=60 * 2**20
        ),
        cost_estimate=pl.CostEstimate(
            flops=2 * rows_all * tile * width, bytes_accessed=2 * tile * width, transcendentals=0
        ),
    )(ids, hidden, base, down, up)


def solution(mesh):
    return jax.shard_map(
        functools.partial(on_device, mesh.shape["gx"]),
        mesh=mesh,
        in_specs=(
            P(("groups", "gx"), "gy"),
            P("gx", "gy"),
            P("gy", "gx", None),
            P("gx", None, "gy"),
            P(("groups", "gx")),
        ),
        out_specs=P(("groups", "gx"), "gy"),
        check_vma=False,
    )
```

```python
import functools

import jax
import jax.numpy as jnp
from jax import lax
from jax.experimental import pallas as pl
from jax.experimental.pallas import tpu as pltpu
from jax.sharding import PartitionSpec as P

UPDATE_SCALE = 0.5
FOLD = 8
ROW_PAD = 32
MESH = pl.DeviceIdType.MESH
F32 = jnp.float32
BF16 = jnp.bfloat16


def kernel(
    n, capacity, rank, chunks,
    ids_ref, hid_ref, w_ref, down_ref, up_ref, out_ref,
    w_v, down_v, up_v, ids_all, tile_in, rows, folded, packed, slots_in,
    half_out, half_in, part, y_in, z_in, low_slots, d_own, d_out, d_in,
    w_sem, ad_sem, id_send, id_recv, t_send, t_recv, f_send, l_send, l_recv,
    h_send, h_recv, y_send, y_recv, z_send, z_recv, d_send, d_recv,
):
    g, c, s = lax.axis_index("groups"), lax.axis_index("gx"), lax.axis_index("gy")
    m = n // 2
    zz, yy = c // 2, c % 2
    row_dev, width = hid_ref.shape
    tile = w_ref.shape[0]
    fold_width = width // FOLD
    slot_rows = capacity * FOLD
    cc = width // chunks
    primary = (c // m) == s

    def peer(cx):
        return (g, cx, s)

    partner = (g, c, 1 - s)

    def w_copy(k):
        cols = pl.ds(pl.multiple_of(k * cc, cc), cc)
        return pltpu.make_async_copy(w_ref.at[:, cols], w_v.at[:, cols], w_sem.at[k])

    down_copy = pltpu.make_async_copy(down_ref, down_v, ad_sem.at[0])
    up_copy = pltpu.make_async_copy(up_ref, up_v, ad_sem.at[1])

    barrier = pltpu.get_barrier_semaphore()
    for j in range(1, n):
        pl.semaphore_signal(barrier, inc=1, device_id=peer((c + j) % n), device_id_type=MESH)
    pl.semaphore_signal(barrier, inc=1, device_id=partner, device_id_type=MESH)

    @pl.loop(0, chunks)
    def _(k):
        w_copy(k).start()

    down_copy.start()
    up_copy.start()

    pl.semaphore_wait(barrier, n)

    def id_copy(dst, j):
        return pltpu.make_async_remote_copy(
            ids_ref, ids_all.at[c], id_send.at[j], id_recv.at[c], device_id=peer(dst),
            device_id_type=MESH,
        )

    def tile_copy(j):
        t = s * m + j
        cols = pl.ds(pl.multiple_of(j * tile, tile), tile)
        return t, pltpu.make_async_remote_copy(
            hid_ref.at[:, cols], tile_in.at[c], t_send.at[j], t_recv.at[c],
            device_id=peer(t), device_id_type=MESH,
        )

    own_cols = pl.ds(pl.multiple_of((c - s * m) * tile, tile), tile)

    @pl.loop(0, m)
    def _(j):
        t, copy = tile_copy(j)

        @pl.when(t != c)
        def _():
            copy.start()

    @pl.when(primary)
    def _():
        pltpu.make_async_copy(hid_ref.at[:, own_cols], tile_in.at[c], t_recv.at[c]).start()

    @pl.loop(1, n)
    def _(j):
        id_copy((c + j) % n, j).start()

    own_ids = pltpu.make_async_copy(ids_ref, ids_all.at[c], id_recv.at[c])
    own_ids.start()

    k_pad = FOLD * ROW_PAD
    owner_row = ids_ref[1:2, :]
    lane = lax.broadcasted_iota(jnp.int32, (ROW_PAD, k_pad), 1)
    sub = lax.broadcasted_iota(jnp.int32, (ROW_PAD, k_pad), 0)
    owner_all = jnp.broadcast_to(owner_row, (ROW_PAD, k_pad))
    owner_col = jnp.sum(jnp.where(lane == sub, owner_all, 0.0), axis=1, keepdims=True)
    earlier = (owner_all == owner_col) & (sub < (lane & (ROW_PAD - 1)))
    rank_row = jnp.sum(jnp.where(earlier, 1.0, 0.0), axis=0, keepdims=True)
    code_row = jnp.where(owner_row >= 0.0, owner_row * capacity + rank_row, -1.0)
    code_row = code_row.astype(jnp.int32)
    total_rows = n * slot_rows
    big_row = lax.broadcasted_iota(jnp.int32, (total_rows, k_pad), 0)
    big_lane = lax.broadcasted_iota(jnp.int32, (total_rows, k_pad), 1)
    placer = ((big_row >> 3) == code_row) & ((big_row & 7) == (big_lane >> 5))
    placer = jnp.where(placer, 1.0, 0.0).astype(BF16)
    for q in range(FOLD):
        block = hid_ref[:, q * fold_width:(q + 1) * fold_width].astype(F32)
        block = jnp.concatenate(
            [block, jnp.zeros((ROW_PAD - row_dev, fold_width), F32)], axis=0
        )
        folded[q * ROW_PAD:(q + 1) * ROW_PAD, :] = block.astype(BF16)
    sent = jnp.dot(placer, folded[...], preferred_element_type=F32).astype(BF16)
    for d in range(n):
        packed[d] = sent[d * slot_rows:(d + 1) * slot_rows, :]

    def slot_copy(dst, j):
        return pltpu.make_async_remote_copy(
            packed.at[dst], slots_in.at[c], l_send.at[j], l_recv.at[c], device_id=peer(dst),
            device_id_type=MESH,
        )

    @pl.loop(0, m)
    def _(j):
        t, copy = tile_copy(j)

        @pl.when(t != c)
        def _():
            copy.wait_send()

    @pl.loop(1, n)
    def _(j):
        slot_copy((c + j) % n, j).start()

    own_slots = pltpu.make_async_copy(packed.at[c], slots_in.at[c], l_recv.at[c])
    own_slots.start()

    def forward(src):
        return pltpu.make_async_remote_copy(
            tile_in.at[src], tile_in.at[src], f_send.at[src], t_recv.at[src],
            device_id=partner, device_id_type=MESH,
        )

    @pl.loop(0, n)
    def _(j):
        src = (c + j) % n
        forward(src).wait_recv()

        @pl.when(primary)
        def _():
            forward(src).start()

    for p in range(m):
        pair = jnp.concatenate([tile_in[2 * p].astype(F32), tile_in[2 * p + 1].astype(F32)], axis=0)
        rows[2 * row_dev * p:2 * row_dev * (p + 1), :] = pair.astype(BF16)

    def columns(k):
        return pl.ds(pl.multiple_of(k * cc, cc), cc)

    def y_copy(k):
        cols = columns(k)
        return pltpu.make_async_remote_copy(
            part.at[1 - yy, :, :, cols], y_in.at[:, :, cols], y_send.at[k], y_recv.at[k],
            device_id=peer(zz * 2 + 1 - yy), device_id_type=MESH,
        )

    early = chunks // 2

    @pl.loop(0, chunks)
    def _(k):
        w_copy(k).wait()
        cols = columns(k)
        acc = jnp.dot(rows[...], w_v[:, cols], preferred_element_type=F32)
        for b in range(n):
            part[b % 2, b // 2, :, cols] = acc[b * row_dev:(b + 1) * row_dev, :].astype(BF16)

        @pl.when(k < early)
        def _():
            y_copy(k).start()

    @pl.loop(1, n)
    def _(j):
        src = (c + j) % n
        pltpu.make_async_remote_copy(
            packed.at[src], slots_in.at[src], l_send.at[j], l_recv.at[src],
            device_id=peer(src), device_id_type=MESH,
        ).wait_recv()

    own_slots.wait()
    down_copy.wait()
    slots = slots_in[...].reshape(total_rows, fold_width)
    cols_rank = down_ref.shape[0]
    fold_of = lax.broadcasted_iota(jnp.int32, (total_rows, cols_rank), 0) & 7
    low = jnp.zeros((total_rows, cols_rank), F32)
    for q in range(FOLD):
        term = lax.dot_general(
            slots, down_v[:, q * fold_width:(q + 1) * fold_width], (((1,), (1,)), ((), ())),
            preferred_element_type=F32,
        )
        low = low + jnp.where(fold_of == q, term, 0.0)
    slot_total = n * capacity
    half = jnp.sum(low.reshape(slot_total, FOLD, cols_rank), axis=1)
    half_out[...] = half
    half_copy = pltpu.make_async_remote_copy(
        half_out, half_in, h_send, h_recv, device_id=partner, device_id_type=MESH
    )
    half_copy.start()

    @pl.loop(1, n)
    def _(j):
        src = (c + j) % n
        pltpu.make_async_remote_copy(
            ids_ref, ids_all.at[src], id_send.at[j], id_recv.at[src], device_id=peer(src),
            device_id_type=MESH,
        ).wait_recv()

    own_ids.wait()
    sub = lax.broadcasted_iota(jnp.int32, (row_dev, 128), 0)
    lane = lax.broadcasted_iota(jnp.int32, (row_dev, 128), 1)
    side = m * capacity

    def slot_of(b):
        id_row = jnp.broadcast_to(ids_all[b, 0:1, 0:128], (row_dev, 128))
        owner_row = jnp.broadcast_to(ids_all[b, 1:2, 0:128], (row_dev, 128))
        id_col = jnp.sum(jnp.where(lane == sub, id_row, 0.0), axis=1, keepdims=True)
        owner_col = jnp.sum(jnp.where(lane == sub, owner_row, 0.0), axis=1, keepdims=True)
        earlier = (owner_row == owner_col) & (lane < sub)
        rank_col = jnp.sum(jnp.where(earlier, 1.0, 0.0), axis=1, keepdims=True)
        return id_col, owner_col, rank_col

    me = c.astype(F32)
    other = (zz * 2 + 1 - yy).astype(F32)
    slot_lane = lax.broadcasted_iota(jnp.int32, (row_dev, slot_total), 1).astype(F32)
    side_lane = lax.broadcasted_iota(jnp.int32, (row_dev, side), 1).astype(F32)
    hit_list, id_list, side_list, own_list, other_list = [], [], [], [], []
    for b in range(n):
        id_col, owner_col, rank_col = slot_of(b)
        mine = owner_col == me
        slot_col = jnp.where(mine, b * capacity + rank_col, -1.0)
        hit_list.append(jnp.where(slot_lane == slot_col, 1.0, 0.0))
        slot_col = jnp.where(mine, (b % 2) * side + (b // 2) * capacity + rank_col, -1.0)
        side_list.append(jnp.where(slot_lane == slot_col, 1.0, 0.0))
        id_list.append(jnp.broadcast_to(id_col, (row_dev, cols_rank)))
    for b in range(m):
        id_col, owner_col, rank_col = slot_of(2 * b + yy)
        at = b * capacity + rank_col
        own_list.append(jnp.where(side_lane == jnp.where(owner_col == me, at, -1.0), 1.0, 0.0))
        other_list.append(jnp.where(side_lane == jnp.where(owner_col == other, at, -1.0), 1.0, 0.0))
    sides = jnp.concatenate(side_list, axis=0).astype(BF16)
    own_hits = jnp.concatenate(own_list, axis=0).astype(BF16)
    other_hits = jnp.concatenate(other_list, axis=0).astype(BF16)
    hits = jnp.concatenate(hit_list, axis=0).astype(BF16)
    ids = jnp.concatenate(id_list, axis=0)
    half_copy.wait()
    shrink = (half + half_in[...]).astype(BF16)
    spread = jnp.dot(hits, shrink, preferred_element_type=F32)
    first = (lax.broadcasted_iota(jnp.int32, ids.shape, 1) + c * cols_rank).astype(F32)
    off = first - rank * ids
    low_rows = jnp.where((off >= 0.0) & (off < rank), spread * UPDATE_SCALE, 0.0).astype(BF16)

    by_side = lax.dot_general(
        sides, low_rows, (((0,), (0,)), ((), ())), preferred_element_type=F32
    )
    for y in range(2):
        low_slots[y] = by_side[y * side:(y + 1) * side, :].astype(BF16)

    up_copy.wait()

    def d_copy(k):
        cols = columns(k)
        return pltpu.make_async_remote_copy(
            d_out.at[:, cols], d_in.at[:, cols], d_send.at[k], d_recv.at[k],
            device_id=peer(zz * 2 + 1 - yy), device_id_type=MESH,
        )

    @pl.loop(0, chunks)
    def _(k):
        cols = columns(k)
        d_out[:, cols] = jnp.dot(
            low_slots[1 - yy], up_v[:, cols], preferred_element_type=F32
        ).astype(BF16)
        d_copy(k).start()

        @pl.when(k % 2 == 1)
        def _():
            y_copy(early + k // 2).start()

        d_own[:, cols] = jnp.dot(
            low_slots[yy], up_v[:, cols], preferred_element_type=F32
        ).astype(BF16)

    def z_copy(k, j):
        to = (zz + j) % m
        cols = columns(k)
        return pltpu.make_async_remote_copy(
            part.at[yy, to, :, cols], z_in.at[zz, :, cols], z_send.at[k, j], z_recv.at[k, zz],
            device_id=peer(to * 2 + yy), device_id_type=MESH,
        )

    @pl.loop(0, chunks)
    def _(k):
        cols = columns(k)
        y_copy(k).wait_recv()
        d_copy(k).wait_recv()
        delta = jnp.dot(own_hits, d_own[:, cols], preferred_element_type=F32)
        delta = delta + jnp.dot(other_hits, d_in[:, cols], preferred_element_type=F32)
        for b in range(m):
            total = part[yy, b, :, cols].astype(F32) + y_in[b, :, cols].astype(F32)
            total = total + delta[b * row_dev:(b + 1) * row_dev, :]
            part[yy, b, :, cols] = total.astype(BF16)

        @pl.loop(1, m)
        def _(j):
            z_copy(k, j).start()

    @pl.loop(0, chunks)
    def _(k):
        cols = columns(k)
        total = part[yy, zz, :, cols].astype(F32)
        for j in range(1, m):
            src = (zz + j) % m
            pltpu.make_async_remote_copy(
                part.at[yy, src, :, cols], z_in.at[src, :, cols], z_send.at[k, j],
                z_recv.at[k, src], device_id=peer(src * 2 + yy), device_id_type=MESH,
            ).wait_recv()
            total = total + z_in[src, :, cols].astype(F32)
        out_ref[:, cols] = total.astype(out_ref.dtype)

    @pl.loop(0, chunks)
    def _(k):
        y_copy(k).wait_send()
        d_copy(k).wait_send()

        @pl.loop(1, m)
        def _(j):
            z_copy(k, j).wait_send()

    @pl.loop(1, n)
    def _(j):
        id_copy((c + j) % n, j).wait_send()
        slot_copy((c + j) % n, j).wait_send()

    @pl.when(primary)
    def _():
        @pl.loop(0, n)
        def _(src):
            forward(src).wait_send()


def on_device(n, hidden, base, down, up, index):
    row_dev, width = hidden.shape
    tile = base.shape[0]
    per_owner, rank = up.shape[0], up.shape[1]
    joined = per_owner * rank
    down = down.transpose(1, 2, 0).reshape(joined, width)
    up = up.reshape(joined, width)
    capacity = max(2, 2 * row_dev // n)
    chunks = 16
    m = n // 2
    padded = jnp.pad(index, (0, ROW_PAD - row_dev), constant_values=-1)
    owner = jnp.where(padded < 0, -1, padded // per_owner)
    first = (jnp.arange(8) == 0)[:, None]
    ids = jnp.where(first, jnp.tile(padded, FOLD)[None, :], jnp.tile(owner, FOLD)[None, :])
    ids = ids.astype(F32)
    slot_rows = capacity * FOLD
    dma = pltpu.SemaphoreType.DMA
    vmem = pl.BlockSpec(memory_space=pltpu.VMEM)
    anywhere = pl.BlockSpec(memory_space=pl.ANY)
    rows_all = n * row_dev
    return pl.pallas_call(
        functools.partial(kernel, n, capacity, rank, chunks),
        out_shape=jax.ShapeDtypeStruct((row_dev, width), BF16),
        in_specs=[vmem, vmem, anywhere, anywhere, anywhere],
        out_specs=vmem,
        scratch_shapes=[
            pltpu.VMEM((tile, width), BF16),
            pltpu.VMEM((joined, width), BF16),
            pltpu.VMEM((joined, width), BF16),
            pltpu.VMEM((n, 8, FOLD * ROW_PAD), F32),
            pltpu.VMEM((n, row_dev, tile), BF16),
            pltpu.VMEM((rows_all, tile), BF16),
            pltpu.VMEM((FOLD * ROW_PAD, width // FOLD), BF16),
            pltpu.VMEM((n, slot_rows, width // FOLD), BF16),
            pltpu.VMEM((n, slot_rows, width // FOLD), BF16),
            pltpu.VMEM((n * capacity, joined), F32),
            pltpu.VMEM((n * capacity, joined), F32),
            pltpu.VMEM((2, m, row_dev, width), BF16),
            pltpu.VMEM((m, row_dev, width), BF16),
            pltpu.VMEM((m, row_dev, width), BF16),
            pltpu.VMEM((2, m * capacity, joined), BF16),
            pltpu.VMEM((m * capacity, width), BF16),
            pltpu.VMEM((m * capacity, width), BF16),
            pltpu.VMEM((m * capacity, width), BF16),
            dma((chunks,)),
            dma((2,)),
            dma((n,)), dma((n,)),
            dma((m,)), dma((n,)),
            dma((n,)),
            dma((n,)), dma((n,)),
            dma, dma,
            dma((chunks,)), dma((chunks,)),
            dma((chunks, m)), dma((chunks, m)),
            dma((chunks,)), dma((chunks,)),
        ],
        compiler_params=pltpu.CompilerParams(
            collective_id=0, has_side_effects=True, vmem_limit_bytes=60 * 2**20
        ),
        cost_estimate=pl.CostEstimate(
            flops=2 * rows_all * tile * width, bytes_accessed=2 * tile * width, transcendentals=0
        ),
    )(ids, hidden, base, down, up)


def solution(mesh):
    return jax.shard_map(
        functools.partial(on_device, mesh.shape["gx"]),
        mesh=mesh,
        in_specs=(
            P(("groups", "gx"), "gy"),
            P("gx", "gy"),
            P("gy", "gx", None),
            P("gx", None, "gy"),
            P(("groups", "gx")),
        ),
        out_specs=P(("groups", "gx"), "gy"),
        check_vma=False,
    )
```

```python
import functools

import jax
import jax.numpy as jnp
from jax import lax
from jax.experimental import pallas as pl
from jax.experimental.pallas import tpu as pltpu
from jax.sharding import PartitionSpec as P

UPDATE_SCALE = 0.5
FOLD = 8
ROW_PAD = 32
MESH = pl.DeviceIdType.MESH
F32 = jnp.float32
BF16 = jnp.bfloat16


def kernel(
    n, capacity, rank, chunks,
    ids_ref, hid_ref, w_ref, down_ref, up_ref, out_ref,
    w_v, down_v, up_v, ids_all, tile_in, rows, folded, packed, slots_in,
    half_out, half_in, part, y_in, up_in, dn_in, low_slots, d_own, d_out, d_in,
    w_sem, ad_sem, id_send, id_recv, t_send, t_recv, f_send, l_send, l_recv,
    h_send, h_recv, y_send, y_recv, u_send, u_recv, n_send, n_recv, d_send, d_recv,
):
    g, c, s = lax.axis_index("groups"), lax.axis_index("gx"), lax.axis_index("gy")
    m = n // 2
    zz, yy = c // 2, c % 2
    row_dev, width = hid_ref.shape
    tile = w_ref.shape[0]
    fold_width = width // FOLD
    slot_rows = capacity * FOLD
    cc = width // chunks
    primary = (c // m) == s

    def peer(cx):
        return (g, cx, s)

    partner = (g, c, 1 - s)

    def w_copy(k):
        cols = pl.ds(pl.multiple_of(k * cc, cc), cc)
        return pltpu.make_async_copy(w_ref.at[:, cols], w_v.at[:, cols], w_sem.at[k])

    down_copy = pltpu.make_async_copy(down_ref, down_v, ad_sem.at[0])
    up_copy = pltpu.make_async_copy(up_ref, up_v, ad_sem.at[1])

    barrier = pltpu.get_barrier_semaphore()
    for j in range(1, n):
        pl.semaphore_signal(barrier, inc=1, device_id=peer((c + j) % n), device_id_type=MESH)
    pl.semaphore_signal(barrier, inc=1, device_id=partner, device_id_type=MESH)

    @pl.loop(0, chunks)
    def _(k):
        w_copy(k).start()

    down_copy.start()
    up_copy.start()

    pl.semaphore_wait(barrier, n)

    def id_copy(dst, j):
        return pltpu.make_async_remote_copy(
            ids_ref, ids_all.at[c], id_send.at[j], id_recv.at[c], device_id=peer(dst),
            device_id_type=MESH,
        )

    def tile_copy(j):
        t = s * m + j
        cols = pl.ds(pl.multiple_of(j * tile, tile), tile)
        return t, pltpu.make_async_remote_copy(
            hid_ref.at[:, cols], tile_in.at[c], t_send.at[j], t_recv.at[c],
            device_id=peer(t), device_id_type=MESH,
        )

    own_cols = pl.ds(pl.multiple_of((c - s * m) * tile, tile), tile)

    @pl.loop(0, m)
    def _(j):
        t, copy = tile_copy(j)

        @pl.when(t != c)
        def _():
            copy.start()

    @pl.when(primary)
    def _():
        pltpu.make_async_copy(hid_ref.at[:, own_cols], tile_in.at[c], t_recv.at[c]).start()

    @pl.loop(1, n)
    def _(j):
        id_copy((c + j) % n, j).start()

    own_ids = pltpu.make_async_copy(ids_ref, ids_all.at[c], id_recv.at[c])
    own_ids.start()

    k_pad = FOLD * ROW_PAD
    owner_row = ids_ref[1:2, :]
    lane = lax.broadcasted_iota(jnp.int32, (ROW_PAD, k_pad), 1)
    sub = lax.broadcasted_iota(jnp.int32, (ROW_PAD, k_pad), 0)
    owner_all = jnp.broadcast_to(owner_row, (ROW_PAD, k_pad))
    owner_col = jnp.sum(jnp.where(lane == sub, owner_all, 0.0), axis=1, keepdims=True)
    earlier = (owner_all == owner_col) & (sub < (lane & (ROW_PAD - 1)))
    rank_row = jnp.sum(jnp.where(earlier, 1.0, 0.0), axis=0, keepdims=True)
    code_row = jnp.where(owner_row >= 0.0, owner_row * capacity + rank_row, -1.0)
    code_row = code_row.astype(jnp.int32)
    total_rows = n * slot_rows
    big_row = lax.broadcasted_iota(jnp.int32, (total_rows, k_pad), 0)
    big_lane = lax.broadcasted_iota(jnp.int32, (total_rows, k_pad), 1)
    placer = ((big_row >> 3) == code_row) & ((big_row & 7) == (big_lane >> 5))
    placer = jnp.where(placer, 1.0, 0.0).astype(BF16)
    for q in range(FOLD):
        block = hid_ref[:, q * fold_width:(q + 1) * fold_width].astype(F32)
        block = jnp.concatenate(
            [block, jnp.zeros((ROW_PAD - row_dev, fold_width), F32)], axis=0
        )
        folded[q * ROW_PAD:(q + 1) * ROW_PAD, :] = block.astype(BF16)
    sent = jnp.dot(placer, folded[...], preferred_element_type=F32).astype(BF16)
    for d in range(n):
        packed[d] = sent[d * slot_rows:(d + 1) * slot_rows, :]

    def slot_copy(dst, j):
        return pltpu.make_async_remote_copy(
            packed.at[dst], slots_in.at[c], l_send.at[j], l_recv.at[c], device_id=peer(dst),
            device_id_type=MESH,
        )

    @pl.loop(0, m)
    def _(j):
        t, copy = tile_copy(j)

        @pl.when(t != c)
        def _():
            copy.wait_send()

    @pl.loop(1, n)
    def _(j):
        slot_copy((c + j) % n, j).start()

    own_slots = pltpu.make_async_copy(packed.at[c], slots_in.at[c], l_recv.at[c])
    own_slots.start()

    def forward(src):
        return pltpu.make_async_remote_copy(
            tile_in.at[src], tile_in.at[src], f_send.at[src], t_recv.at[src],
            device_id=partner, device_id_type=MESH,
        )

    @pl.loop(0, n)
    def _(j):
        src = (c + j) % n
        forward(src).wait_recv()

        @pl.when(primary)
        def _():
            forward(src).start()

    for p in range(m):
        pair = jnp.concatenate([tile_in[2 * p].astype(F32), tile_in[2 * p + 1].astype(F32)], axis=0)
        rows[2 * row_dev * p:2 * row_dev * (p + 1), :] = pair.astype(BF16)

    def columns(k):
        return pl.ds(pl.multiple_of(k * cc, cc), cc)

    def y_copy(k):
        cols = columns(k)
        return pltpu.make_async_remote_copy(
            part.at[1 - yy, :, :, cols], y_in.at[:, :, cols], y_send.at[k], y_recv.at[k],
            device_id=peer(zz * 2 + 1 - yy), device_id_type=MESH,
        )

    early = chunks // 2

    @pl.loop(0, chunks)
    def _(k):
        w_copy(k).wait()
        cols = columns(k)
        acc = jnp.dot(rows[...], w_v[:, cols], preferred_element_type=F32)
        for b in range(n):
            part[b % 2, b // 2, :, cols] = acc[b * row_dev:(b + 1) * row_dev, :].astype(BF16)

        @pl.when(k < early)
        def _():
            y_copy(k).start()

    @pl.loop(1, n)
    def _(j):
        src = (c + j) % n
        pltpu.make_async_remote_copy(
            packed.at[src], slots_in.at[src], l_send.at[j], l_recv.at[src],
            device_id=peer(src), device_id_type=MESH,
        ).wait_recv()

    own_slots.wait()
    down_copy.wait()
    slots = slots_in[...].reshape(total_rows, fold_width)
    cols_rank = down_ref.shape[0]
    fold_of = lax.broadcasted_iota(jnp.int32, (total_rows, cols_rank), 0) & 7
    low = jnp.zeros((total_rows, cols_rank), F32)
    for q in range(FOLD):
        term = lax.dot_general(
            slots, down_v[:, q * fold_width:(q + 1) * fold_width], (((1,), (1,)), ((), ())),
            preferred_element_type=F32,
        )
        low = low + jnp.where(fold_of == q, term, 0.0)
    slot_total = n * capacity
    half = jnp.sum(low.reshape(slot_total, FOLD, cols_rank), axis=1)
    half_out[...] = half
    half_copy = pltpu.make_async_remote_copy(
        half_out, half_in, h_send, h_recv, device_id=partner, device_id_type=MESH
    )
    half_copy.start()

    @pl.loop(1, n)
    def _(j):
        src = (c + j) % n
        pltpu.make_async_remote_copy(
            ids_ref, ids_all.at[src], id_send.at[j], id_recv.at[src], device_id=peer(src),
            device_id_type=MESH,
        ).wait_recv()

    own_ids.wait()
    sub = lax.broadcasted_iota(jnp.int32, (row_dev, 128), 0)
    lane = lax.broadcasted_iota(jnp.int32, (row_dev, 128), 1)
    side = m * capacity

    def slot_of(b):
        id_row = jnp.broadcast_to(ids_all[b, 0:1, 0:128], (row_dev, 128))
        owner_row = jnp.broadcast_to(ids_all[b, 1:2, 0:128], (row_dev, 128))
        id_col = jnp.sum(jnp.where(lane == sub, id_row, 0.0), axis=1, keepdims=True)
        owner_col = jnp.sum(jnp.where(lane == sub, owner_row, 0.0), axis=1, keepdims=True)
        earlier = (owner_row == owner_col) & (lane < sub)
        rank_col = jnp.sum(jnp.where(earlier, 1.0, 0.0), axis=1, keepdims=True)
        return id_col, owner_col, rank_col

    me = c.astype(F32)
    other = (zz * 2 + 1 - yy).astype(F32)
    slot_lane = lax.broadcasted_iota(jnp.int32, (row_dev, slot_total), 1).astype(F32)
    side_lane = lax.broadcasted_iota(jnp.int32, (row_dev, side), 1).astype(F32)
    hit_list, id_list, side_list, own_list, other_list = [], [], [], [], []
    for b in range(n):
        id_col, owner_col, rank_col = slot_of(b)
        mine = owner_col == me
        slot_col = jnp.where(mine, b * capacity + rank_col, -1.0)
        hit_list.append(jnp.where(slot_lane == slot_col, 1.0, 0.0))
        slot_col = jnp.where(mine, (b % 2) * side + (b // 2) * capacity + rank_col, -1.0)
        side_list.append(jnp.where(slot_lane == slot_col, 1.0, 0.0))
        id_list.append(jnp.broadcast_to(id_col, (row_dev, cols_rank)))
    for b in range(m):
        id_col, owner_col, rank_col = slot_of(2 * b + yy)
        at = b * capacity + rank_col
        own_list.append(jnp.where(side_lane == jnp.where(owner_col == me, at, -1.0), 1.0, 0.0))
        other_list.append(jnp.where(side_lane == jnp.where(owner_col == other, at, -1.0), 1.0, 0.0))
    sides = jnp.concatenate(side_list, axis=0).astype(BF16)
    own_hits = jnp.concatenate(own_list, axis=0).astype(BF16)
    other_hits = jnp.concatenate(other_list, axis=0).astype(BF16)
    hits = jnp.concatenate(hit_list, axis=0).astype(BF16)
    ids = jnp.concatenate(id_list, axis=0)
    half_copy.wait()
    shrink = (half + half_in[...]).astype(BF16)
    spread = jnp.dot(hits, shrink, preferred_element_type=F32)
    first = (lax.broadcasted_iota(jnp.int32, ids.shape, 1) + c * cols_rank).astype(F32)
    off = first - rank * ids
    low_rows = jnp.where((off >= 0.0) & (off < rank), spread * UPDATE_SCALE, 0.0).astype(BF16)

    by_side = lax.dot_general(
        sides, low_rows, (((0,), (0,)), ((), ())), preferred_element_type=F32
    )
    for y in range(2):
        low_slots[y] = by_side[y * side:(y + 1) * side, :].astype(BF16)

    up_copy.wait()

    def d_copy(k):
        cols = columns(k)
        return pltpu.make_async_remote_copy(
            d_out.at[:, cols], d_in.at[:, cols], d_send.at[k], d_recv.at[k],
            device_id=peer(zz * 2 + 1 - yy), device_id_type=MESH,
        )

    @pl.loop(0, chunks)
    def _(k):
        cols = columns(k)
        d_out[:, cols] = jnp.dot(
            low_slots[1 - yy], up_v[:, cols], preferred_element_type=F32
        ).astype(BF16)
        d_copy(k).start()

        @pl.when(k % 2 == 1)
        def _():
            y_copy(early + k // 2).start()

        d_own[:, cols] = jnp.dot(
            low_slots[yy], up_v[:, cols], preferred_element_type=F32
        ).astype(BF16)

    def z_copy(k, b, step, buffer, send, recv):
        cols = columns(k)
        return pltpu.make_async_remote_copy(
            buffer.at[b, :, cols], buffer.at[b, :, cols], send.at[k, b], recv.at[k, b],
            device_id=peer((zz + step + m) % m * 2 + yy), device_id_type=MESH,
        )

    def up_copy_of(k, b):
        return z_copy(k, b, 1, up_in, u_send, u_recv)

    def dn_copy_of(k, b):
        return z_copy(k, b, -1, dn_in, n_send, n_recv)

    def pass_on(k, b, copy_of, buffer, starts):
        cols = columns(k)
        own = part[yy, b, :, cols]

        @pl.when(starts)
        def _():
            buffer[b, :, cols] = own

        @pl.when(jnp.logical_not(starts))
        def _():
            copy_of(k, b).wait_recv()
            total = own.astype(F32) + buffer[b, :, cols].astype(F32)
            buffer[b, :, cols] = total.astype(BF16)

        copy_of(k, b).start()

    lag = 2

    @pl.loop(0, chunks + lag * (m - 1))
    def _(i):
        @pl.when(i < chunks)
        def _():
            cols = columns(i)
            y_copy(i).wait_recv()
            d_copy(i).wait_recv()
            delta = jnp.dot(own_hits, d_own[:, cols], preferred_element_type=F32)
            delta = delta + jnp.dot(other_hits, d_in[:, cols], preferred_element_type=F32)
            for b in range(m):
                total = part[yy, b, :, cols].astype(F32) + y_in[b, :, cols].astype(F32)
                total = total + delta[b * row_dev:(b + 1) * row_dev, :]
                part[yy, b, :, cols] = total.astype(BF16)

        k_up = i - lag * zz

        @pl.when((k_up >= 0) & (k_up < chunks))
        def _():
            @pl.loop(zz + 1, m)
            def _(b):
                pass_on(k_up, b, up_copy_of, up_in, zz == 0)

        k_dn = i - lag * (m - 1 - zz)

        @pl.when((k_dn >= 0) & (k_dn < chunks))
        def _():
            @pl.loop(0, zz)
            def _(b):
                pass_on(k_dn, b, dn_copy_of, dn_in, zz == m - 1)

    @pl.loop(0, chunks)
    def _(k):
        cols = columns(k)
        own = part[yy, zz, :, cols].astype(F32)

        @pl.when(zz > 0)
        def _():
            up_copy_of(k, zz).wait_recv()

        @pl.when(zz < m - 1)
        def _():
            dn_copy_of(k, zz).wait_recv()

        @pl.when(zz == 0)
        def _():
            out_ref[:, cols] = (own + dn_in[zz, :, cols].astype(F32)).astype(BF16)

        @pl.when(zz == m - 1)
        def _():
            out_ref[:, cols] = (own + up_in[zz, :, cols].astype(F32)).astype(BF16)

        @pl.when((zz > 0) & (zz < m - 1))
        def _():
            total = own + dn_in[zz, :, cols].astype(F32) + up_in[zz, :, cols].astype(F32)
            out_ref[:, cols] = total.astype(BF16)

    @pl.loop(0, chunks)
    def _(k):
        y_copy(k).wait_send()
        d_copy(k).wait_send()

        @pl.loop(zz + 1, m)
        def _(b):
            up_copy_of(k, b).wait_send()

        @pl.loop(0, zz)
        def _(b):
            dn_copy_of(k, b).wait_send()

    @pl.loop(1, n)
    def _(j):
        id_copy((c + j) % n, j).wait_send()
        slot_copy((c + j) % n, j).wait_send()

    @pl.when(primary)
    def _():
        @pl.loop(0, n)
        def _(src):
            forward(src).wait_send()


def on_device(n, hidden, base, down, up, index):
    row_dev, width = hidden.shape
    tile = base.shape[0]
    per_owner, rank = up.shape[0], up.shape[1]
    joined = per_owner * rank
    down = down.transpose(1, 2, 0).reshape(joined, width)
    up = up.reshape(joined, width)
    capacity = max(2, 2 * row_dev // n)
    chunks = 16
    m = n // 2
    padded = jnp.pad(index, (0, ROW_PAD - row_dev), constant_values=-1)
    owner = jnp.where(padded < 0, -1, padded // per_owner)
    first = (jnp.arange(8) == 0)[:, None]
    ids = jnp.where(first, jnp.tile(padded, FOLD)[None, :], jnp.tile(owner, FOLD)[None, :])
    ids = ids.astype(F32)
    slot_rows = capacity * FOLD
    dma = pltpu.SemaphoreType.DMA
    vmem = pl.BlockSpec(memory_space=pltpu.VMEM)
    anywhere = pl.BlockSpec(memory_space=pl.ANY)
    rows_all = n * row_dev
    return pl.pallas_call(
        functools.partial(kernel, n, capacity, rank, chunks),
        out_shape=jax.ShapeDtypeStruct((row_dev, width), BF16),
        in_specs=[vmem, vmem, anywhere, anywhere, anywhere],
        out_specs=vmem,
        scratch_shapes=[
            pltpu.VMEM((tile, width), BF16),
            pltpu.VMEM((joined, width), BF16),
            pltpu.VMEM((joined, width), BF16),
            pltpu.VMEM((n, 8, FOLD * ROW_PAD), F32),
            pltpu.VMEM((n, row_dev, tile), BF16),
            pltpu.VMEM((rows_all, tile), BF16),
            pltpu.VMEM((FOLD * ROW_PAD, width // FOLD), BF16),
            pltpu.VMEM((n, slot_rows, width // FOLD), BF16),
            pltpu.VMEM((n, slot_rows, width // FOLD), BF16),
            pltpu.VMEM((n * capacity, joined), F32),
            pltpu.VMEM((n * capacity, joined), F32),
            pltpu.VMEM((2, m, row_dev, width), BF16),
            pltpu.VMEM((m, row_dev, width), BF16),
            pltpu.VMEM((m, row_dev, width), BF16),
            pltpu.VMEM((m, row_dev, width), BF16),
            pltpu.VMEM((2, m * capacity, joined), BF16),
            pltpu.VMEM((m * capacity, width), BF16),
            pltpu.VMEM((m * capacity, width), BF16),
            pltpu.VMEM((m * capacity, width), BF16),
            dma((chunks,)),
            dma((2,)),
            dma((n,)), dma((n,)),
            dma((m,)), dma((n,)),
            dma((n,)),
            dma((n,)), dma((n,)),
            dma, dma,
            dma((chunks,)), dma((chunks,)),
            dma((chunks, m)), dma((chunks, m)),
            dma((chunks, m)), dma((chunks, m)),
            dma((chunks,)), dma((chunks,)),
        ],
        compiler_params=pltpu.CompilerParams(
            collective_id=0, has_side_effects=True, vmem_limit_bytes=60 * 2**20
        ),
        cost_estimate=pl.CostEstimate(
            flops=2 * rows_all * tile * width, bytes_accessed=2 * tile * width, transcendentals=0
        ),
    )(ids, hidden, base, down, up)


def solution(mesh):
    return jax.shard_map(
        functools.partial(on_device, mesh.shape["gx"]),
        mesh=mesh,
        in_specs=(
            P(("groups", "gx"), "gy"),
            P("gx", "gy"),
            P("gy", "gx", None),
            P("gx", None, "gy"),
            P(("groups", "gx")),
        ),
        out_specs=P(("groups", "gx"), "gy"),
        check_vma=False,
    )
```

```python
import functools

import jax
import jax.numpy as jnp
from jax import lax
from jax.experimental import pallas as pl
from jax.experimental.pallas import tpu as pltpu
from jax.sharding import PartitionSpec as P

UPDATE_SCALE = 0.5
FOLD = 8
ROW_PAD = 32
MESH = pl.DeviceIdType.MESH
F32 = jnp.float32
BF16 = jnp.bfloat16


def kernel(
    n, capacity, rank, chunks,
    ids_ref, hid_ref, w_ref, down_ref, up_ref, out_ref,
    w_v, down_v, up_v, ids_all, tile_in, rows, folded, packed, slots_in,
    half_out, half_in, part, y_in, z_in,
    w_sem, ad_sem, id_send, id_recv, t_send, t_recv, f_send, l_send, l_recv,
    h_send, h_recv, y_send, y_recv, z_send, z_recv,
):
    g, c, s = lax.axis_index("groups"), lax.axis_index("gx"), lax.axis_index("gy")
    m = n // 2
    zz, yy = c // 2, c % 2
    row_dev, width = hid_ref.shape
    tile = w_ref.shape[0]
    fold_width = width // FOLD
    slot_rows = capacity * FOLD
    cc = width // chunks
    primary = (c // m) == s

    def peer(cx):
        return (g, cx, s)

    partner = (g, c, 1 - s)

    def w_copy(k):
        cols = pl.ds(pl.multiple_of(k * cc, cc), cc)
        return pltpu.make_async_copy(w_ref.at[:, cols], w_v.at[:, cols], w_sem.at[k])

    down_copy = pltpu.make_async_copy(down_ref, down_v, ad_sem.at[0])
    up_copy = pltpu.make_async_copy(up_ref, up_v, ad_sem.at[1])

    barrier = pltpu.get_barrier_semaphore()
    for j in range(1, n):
        pl.semaphore_signal(barrier, inc=1, device_id=peer((c + j) % n), device_id_type=MESH)
    pl.semaphore_signal(barrier, inc=1, device_id=partner, device_id_type=MESH)

    @pl.loop(0, chunks)
    def _(k):
        w_copy(k).start()

    down_copy.start()
    up_copy.start()

    pl.semaphore_wait(barrier, n)

    def id_copy(dst, j):
        return pltpu.make_async_remote_copy(
            ids_ref, ids_all.at[c], id_send.at[j], id_recv.at[c], device_id=peer(dst),
            device_id_type=MESH,
        )

    def tile_copy(j):
        t = s * m + j
        cols = pl.ds(pl.multiple_of(j * tile, tile), tile)
        return t, pltpu.make_async_remote_copy(
            hid_ref.at[:, cols], tile_in.at[c], t_send.at[j], t_recv.at[c],
            device_id=peer(t), device_id_type=MESH,
        )

    own_cols = pl.ds(pl.multiple_of((c - s * m) * tile, tile), tile)

    @pl.loop(0, m)
    def _(j):
        t, copy = tile_copy(j)

        @pl.when(t != c)
        def _():
            copy.start()

    @pl.when(primary)
    def _():
        pltpu.make_async_copy(hid_ref.at[:, own_cols], tile_in.at[c], t_recv.at[c]).start()

    @pl.loop(1, n)
    def _(j):
        id_copy((c + j) % n, j).start()

    own_ids = pltpu.make_async_copy(ids_ref, ids_all.at[c], id_recv.at[c])
    own_ids.start()

    k_pad = FOLD * ROW_PAD
    owner_row = ids_ref[1:2, :]
    lane = lax.broadcasted_iota(jnp.int32, (ROW_PAD, k_pad), 1)
    sub = lax.broadcasted_iota(jnp.int32, (ROW_PAD, k_pad), 0)
    owner_all = jnp.broadcast_to(owner_row, (ROW_PAD, k_pad))
    owner_col = jnp.sum(jnp.where(lane == sub, owner_all, 0.0), axis=1, keepdims=True)
    earlier = (owner_all == owner_col) & (sub < (lane & (ROW_PAD - 1)))
    rank_row = jnp.sum(jnp.where(earlier, 1.0, 0.0), axis=0, keepdims=True)
    code_row = jnp.where(owner_row >= 0.0, owner_row * capacity + rank_row, -1.0)
    code_row = code_row.astype(jnp.int32)
    total_rows = n * slot_rows
    big_row = lax.broadcasted_iota(jnp.int32, (total_rows, k_pad), 0)
    big_lane = lax.broadcasted_iota(jnp.int32, (total_rows, k_pad), 1)
    placer = ((big_row >> 3) == code_row) & ((big_row & 7) == (big_lane >> 5))
    placer = jnp.where(placer, 1.0, 0.0).astype(BF16)
    for q in range(FOLD):
        block = hid_ref[:, q * fold_width:(q + 1) * fold_width].astype(F32)
        block = jnp.concatenate(
            [block, jnp.zeros((ROW_PAD - row_dev, fold_width), F32)], axis=0
        )
        folded[q * ROW_PAD:(q + 1) * ROW_PAD, :] = block.astype(BF16)
    sent = jnp.dot(placer, folded[...], preferred_element_type=F32).astype(BF16)
    for d in range(n):
        packed[d] = sent[d * slot_rows:(d + 1) * slot_rows, :]

    def slot_copy(dst, j):
        return pltpu.make_async_remote_copy(
            packed.at[dst], slots_in.at[c], l_send.at[j], l_recv.at[c], device_id=peer(dst),
            device_id_type=MESH,
        )

    @pl.loop(0, m)
    def _(j):
        t, copy = tile_copy(j)

        @pl.when(t != c)
        def _():
            copy.wait_send()

    @pl.loop(1, n)
    def _(j):
        slot_copy((c + j) % n, j).start()

    own_slots = pltpu.make_async_copy(packed.at[c], slots_in.at[c], l_recv.at[c])
    own_slots.start()

    def forward(src):
        return pltpu.make_async_remote_copy(
            tile_in.at[src], tile_in.at[src], f_send.at[src], t_recv.at[src],
            device_id=partner, device_id_type=MESH,
        )

    @pl.loop(0, n)
    def _(j):
        src = (c + j) % n
        forward(src).wait_recv()

        @pl.when(primary)
        def _():
            forward(src).start()

    for p in range(m):
        pair = jnp.concatenate([tile_in[2 * p].astype(F32), tile_in[2 * p + 1].astype(F32)], axis=0)
        rows[2 * row_dev * p:2 * row_dev * (p + 1), :] = pair.astype(BF16)

    def columns(k):
        return pl.ds(pl.multiple_of(k * cc, cc), cc)

    @pl.loop(0, chunks)
    def _(k):
        w_copy(k).wait()
        cols = columns(k)
        acc = jnp.dot(rows[...], w_v[:, cols], preferred_element_type=F32)
        for b in range(n):
            part[b % 2, b // 2, :, cols] = acc[b * row_dev:(b + 1) * row_dev, :].astype(BF16)

    @pl.loop(1, n)
    def _(j):
        src = (c + j) % n
        pltpu.make_async_remote_copy(
            packed.at[src], slots_in.at[src], l_send.at[j], l_recv.at[src],
            device_id=peer(src), device_id_type=MESH,
        ).wait_recv()

    own_slots.wait()
    down_copy.wait()
    slots = slots_in[...].reshape(total_rows, fold_width)
    cols_rank = down_ref.shape[0]
    fold_of = lax.broadcasted_iota(jnp.int32, (total_rows, cols_rank), 0) & 7
    low = jnp.zeros((total_rows, cols_rank), F32)
    for q in range(FOLD):
        term = lax.dot_general(
            slots, down_v[:, q * fold_width:(q + 1) * fold_width], (((1,), (1,)), ((), ())),
            preferred_element_type=F32,
        )
        low = low + jnp.where(fold_of == q, term, 0.0)
    slot_total = n * capacity
    half = jnp.sum(low.reshape(slot_total, FOLD, cols_rank), axis=1)
    half_out[...] = half
    half_copy = pltpu.make_async_remote_copy(
        half_out, half_in, h_send, h_recv, device_id=partner, device_id_type=MESH
    )
    half_copy.start()

    @pl.loop(1, n)
    def _(j):
        src = (c + j) % n
        pltpu.make_async_remote_copy(
            ids_ref, ids_all.at[src], id_send.at[j], id_recv.at[src], device_id=peer(src),
            device_id_type=MESH,
        ).wait_recv()

    own_ids.wait()
    hit_list, id_list = [], []
    sub = lax.broadcasted_iota(jnp.int32, (row_dev, 128), 0)
    lane = lax.broadcasted_iota(jnp.int32, (row_dev, 128), 1)
    slot_lane = lax.broadcasted_iota(jnp.int32, (row_dev, slot_total), 1).astype(F32)
    me = c.astype(F32)
    for b in range(n):
        id_row = jnp.broadcast_to(ids_all[b, 0:1, 0:128], (row_dev, 128))
        owner_row = jnp.broadcast_to(ids_all[b, 1:2, 0:128], (row_dev, 128))
        id_col = jnp.sum(jnp.where(lane == sub, id_row, 0.0), axis=1, keepdims=True)
        owner_col = jnp.sum(jnp.where(lane == sub, owner_row, 0.0), axis=1, keepdims=True)
        earlier = (owner_row == owner_col) & (lane < sub)
        rank_col = jnp.sum(jnp.where(earlier, 1.0, 0.0), axis=1, keepdims=True)
        slot_col = jnp.where(owner_col == me, b * capacity + rank_col, -1.0)
        hit_list.append(jnp.where(slot_lane == slot_col, 1.0, 0.0))
        id_list.append(jnp.broadcast_to(id_col, (row_dev, cols_rank)))
    hits = jnp.concatenate(hit_list, axis=0).astype(BF16)
    ids = jnp.concatenate(id_list, axis=0)
    half_copy.wait()
    shrink = (half + half_in[...]).astype(BF16)
    spread = jnp.dot(hits, shrink, preferred_element_type=F32)
    first = (lax.broadcasted_iota(jnp.int32, ids.shape, 1) + c * cols_rank).astype(F32)
    off = first - rank * ids
    low_rows = jnp.where((off >= 0.0) & (off < rank), spread * UPDATE_SCALE, 0.0).astype(BF16)

    up_copy.wait()

    def y_copy(k):
        cols = columns(k)
        return pltpu.make_async_remote_copy(
            part.at[1 - yy, :, :, cols], y_in.at[:, :, cols], y_send.at[k], y_recv.at[k],
            device_id=peer(zz * 2 + 1 - yy), device_id_type=MESH,
        )

    @pl.loop(0, chunks)
    def _(k):
        cols = columns(k)
        acc = jnp.dot(low_rows, up_v[:, cols], preferred_element_type=F32)
        for b in range(n):
            one = acc[b * row_dev:(b + 1) * row_dev, :]
            part[b % 2, b // 2, :, cols] = (part[b % 2, b // 2, :, cols].astype(F32) + one).astype(BF16)
        y_copy(k).start()

    def z_copy(k, j):
        to = (zz + j) % m
        cols = columns(k)
        return pltpu.make_async_remote_copy(
            part.at[yy, to, :, cols], z_in.at[zz, :, cols], z_send.at[k, j], z_recv.at[k, zz],
            device_id=peer(to * 2 + yy), device_id_type=MESH,
        )

    @pl.loop(0, chunks)
    def _(k):
        cols = columns(k)
        y_copy(k).wait_recv()
        for b in range(m):
            total = part[yy, b, :, cols].astype(F32) + y_in[b, :, cols].astype(F32)
            part[yy, b, :, cols] = total.astype(BF16)

        @pl.loop(1, m)
        def _(j):
            z_copy(k, j).start()

    @pl.loop(0, chunks)
    def _(k):
        cols = columns(k)
        total = part[yy, zz, :, cols].astype(F32)
        for j in range(1, m):
            src = (zz + j) % m
            pltpu.make_async_remote_copy(
                part.at[yy, src, :, cols], z_in.at[src, :, cols], z_send.at[k, j],
                z_recv.at[k, src], device_id=peer(src * 2 + yy), device_id_type=MESH,
            ).wait_recv()
            total = total + z_in[src, :, cols].astype(F32)
        out_ref[:, cols] = total.astype(out_ref.dtype)

    @pl.loop(0, chunks)
    def _(k):
        y_copy(k).wait_send()

        @pl.loop(1, m)
        def _(j):
            z_copy(k, j).wait_send()

    @pl.loop(1, n)
    def _(j):
        id_copy((c + j) % n, j).wait_send()
        slot_copy((c + j) % n, j).wait_send()

    @pl.when(primary)
    def _():
        @pl.loop(0, n)
        def _(src):
            forward(src).wait_send()


def on_device(n, hidden, base, down, up, index):
    row_dev, width = hidden.shape
    tile = base.shape[0]
    per_owner, rank = up.shape[0], up.shape[1]
    joined = per_owner * rank
    down = down.transpose(1, 2, 0).reshape(joined, width)
    up = up.reshape(joined, width)
    capacity = max(2, 2 * row_dev // n)
    chunks = 8
    m = n // 2
    padded = jnp.pad(index, (0, ROW_PAD - row_dev), constant_values=-1)
    owner = jnp.where(padded < 0, -1, padded // per_owner)
    first = (jnp.arange(8) == 0)[:, None]
    ids = jnp.where(first, jnp.tile(padded, FOLD)[None, :], jnp.tile(owner, FOLD)[None, :])
    ids = ids.astype(F32)
    slot_rows = capacity * FOLD
    dma = pltpu.SemaphoreType.DMA
    vmem = pl.BlockSpec(memory_space=pltpu.VMEM)
    anywhere = pl.BlockSpec(memory_space=pl.ANY)
    rows_all = n * row_dev
    return pl.pallas_call(
        functools.partial(kernel, n, capacity, rank, chunks),
        out_shape=jax.ShapeDtypeStruct((row_dev, width), BF16),
        in_specs=[vmem, vmem, anywhere, anywhere, anywhere],
        out_specs=vmem,
        scratch_shapes=[
            pltpu.VMEM((tile, width), BF16),
            pltpu.VMEM((joined, width), BF16),
            pltpu.VMEM((joined, width), BF16),
            pltpu.VMEM((n, 8, FOLD * ROW_PAD), F32),
            pltpu.VMEM((n, row_dev, tile), BF16),
            pltpu.VMEM((rows_all, tile), BF16),
            pltpu.VMEM((FOLD * ROW_PAD, width // FOLD), BF16),
            pltpu.VMEM((n, slot_rows, width // FOLD), BF16),
            pltpu.VMEM((n, slot_rows, width // FOLD), BF16),
            pltpu.VMEM((n * capacity, joined), F32),
            pltpu.VMEM((n * capacity, joined), F32),
            pltpu.VMEM((2, m, row_dev, width), BF16),
            pltpu.VMEM((m, row_dev, width), BF16),
            pltpu.VMEM((m, row_dev, width), BF16),
            dma((chunks,)),
            dma((2,)),
            dma((n,)), dma((n,)),
            dma((m,)), dma((n,)),
            dma((n,)),
            dma((n,)), dma((n,)),
            dma, dma,
            dma((chunks,)), dma((chunks,)),
            dma((chunks, m)), dma((chunks, m)),
        ],
        compiler_params=pltpu.CompilerParams(
            collective_id=0, has_side_effects=True, vmem_limit_bytes=60 * 2**20
        ),
        cost_estimate=pl.CostEstimate(
            flops=2 * rows_all * tile * width, bytes_accessed=2 * tile * width, transcendentals=0
        ),
    )(ids, hidden, base, down, up)


def solution(mesh):
    return jax.shard_map(
        functools.partial(on_device, mesh.shape["gx"]),
        mesh=mesh,
        in_specs=(
            P(("groups", "gx"), "gy"),
            P("gx", "gy"),
            P("gy", "gx", None),
            P("gx", None, "gy"),
            P(("groups", "gx")),
        ),
        out_specs=P(("groups", "gx"), "gy"),
        check_vma=False,
    )
```
